32 devices in a mesh: layer: 2 (over y), dp: 4 (over z), feat: 4 (over x, core).
Axes of the slice: x: 2, y: 2, z: 4, core: 2. Of those that a mesh axis runs over, the one named last changes fastest.
Arguments:
- train_rows: bfloat16 [2048, 4096], P(('layer', 'dp'), 'feat'), parts along dimension 0, may hold values from -6 to 6
- train_labels: int32 [2048, 1], P(('layer', 'dp')), parts along dimension 0, may hold values from 0 to 255
- held_rows: bfloat16 [4096, 4096], P(('layer', 'dp'), 'feat'), parts along dimension 0, may hold values from -6 to 6
- held_labels: int32 [4096], P(('layer', 'dp')), parts along dimension 0, may hold values from 0 to 255
- precision: bfloat16 [6, 4096, 256], P('layer', 'feat'), parts along dimension 0
Outputs:
- pooled_cov: float32 [8192, 4096], P(('layer', 'feat'), 'dp'), parts along dimension 0
- whitened: bfloat16 [4096, 4096], P(('layer', 'dp'), 'feat'), parts along dimension 0
- distance: float32 [4096], P(('layer', 'dp')), parts along dimension 0
The draws below stay inside these ranges and needn't reach their ends.
There are 2 independent parts, one for each index of `layer`. The reference program is written for one: setup_inputs(seed, part) draws one part's arguments, and reference() takes and returns one part's arrays. A program takes and returns all parts, laid end to end along the dimension named above; each array names one. Nothing has to cross between parts.
Inputs may be any that keep to these rules, and one draw needn't show every extreme that they name: `train_labels`: every class has at least one training row.
All inputs are finite; a program needn't handle non-finite values.
Results may differ from the reference program's by a relative error of at most 0.0004.
Values may be sent and summed in bfloat16 or wider, within the bound.
A program may use at most 128 MiB of HBM per device.

```python
import math
import jax
import jax.numpy as jnp
from jax import lax

D = 4096
C = 256
BLK = 256
H_DEV = 512
ROWS = 1024
HELD = 2048


def draw_precision(key, part):
    first, second = jax.random.split(key, 2)
    base = jax.random.normal(first, (3, D, BLK), jnp.float32) * (0.5 / math.sqrt(3 * BLK))
    rows = jnp.arange(D) % BLK
    cols = jnp.arange(BLK)
    diagonal = (rows[:, None] == cols[None, :]).astype(jnp.float32)
    middle = (jnp.arange(3) == 1).astype(jnp.float32)[:, None, None]
    level = jax.random.uniform(second, (D, 1), jnp.float32, 1.0, 2.0)
    band = base + middle * diagonal[None] * level[None]
    return band.astype(jnp.bfloat16)


def set_ends(values, stream_key, least, high):
    index_at = [jax.random.randint(jax.random.fold_in(stream_key, axis), (), 0, length) for axis, length in enumerate(values.shape)]
    longest = values.shape.index(max(values.shape))
    neighbour = index_at[:longest] + [(index_at[longest] + 1) % values.shape[longest]] + index_at[longest + 1:]
    return values.at[tuple(index_at)].set(least).at[tuple(neighbour)].set(high)


def block_scale(key, dims, cuts, low, largest):
    level = 1.0
    for position, shards_of in cuts:
        heights = jax.random.uniform(jax.random.fold_in(jax.random.fold_in(key, 6), position), (shards_of,), jnp.float32, low / len(cuts), largest / len(cuts))
        level = level * jnp.repeat(jnp.exp(heights), dims[position] // shards_of).reshape((-1,) + (1,) * (len(dims) - 1 - position))
    return level


def different_ones(stream_key, rows, count, top, lift):
    ranking = jax.random.permutation(jax.random.fold_in(stream_key, 1), count)
    boost = ranking
    for power in range(3):
        boost = boost * boost // count
    boost = boost * lift // count
    chance = jax.random.randint(jax.random.fold_in(stream_key, 2), (rows, count), 0, 4096) + boost
    sure = jax.random.permutation(jax.random.fold_in(stream_key, 3), rows)[jnp.arange(count) % rows]
    chance = jnp.where(jnp.arange(rows)[:, None] == sure[None, :], 1 << 14, chance)
    merit = chance * count + jnp.arange(count)
    return lax.top_k(merit.astype(jnp.int32), top)[1].astype(jnp.int32)


def bell_draw(stream_key, extent, scale, bound, pieces=(), held_as=jnp.bfloat16):
    factor_of = block_scale(stream_key, extent, pieces, -0.22, 0.18) if pieces else 1.0
    result = jax.random.normal(stream_key, extent, jnp.float32) * scale * factor_of
    return jnp.minimum(jnp.maximum(result, -bound), bound).astype(held_as)


def setup_inputs(seed: int = 0, part: int = 0) -> dict:
    arg_keys = jax.random.split(jax.random.key(seed), 6)
    part_splits = jax.random.split(jax.random.fold_in(arg_keys[5], part), 6)
    return {
        "train_rows": bell_draw(part_splits[0], (ROWS, D), 1.0, 6.0, ((0, 4), (1, 4))),
        "train_labels": different_ones(part_splits[1], ROWS, C, 1, 0),
        "held_rows": bell_draw(part_splits[2], (HELD, D), 1.0, 6.0, ((0, 4), (1, 4))),
        "held_labels": set_ends(jax.random.randint(part_splits[3], (HELD,), 0, C), jax.random.fold_in(part_splits[3], 1), 0, C - 1).astype(jnp.int32),
        "precision": draw_precision(jax.random.fold_in(jax.random.fold_in(arg_keys[5], part), 71), part),
    }


def reference(train_rows, train_labels, held_rows, held_labels, precision):
    classes = jnp.arange(C, dtype=jnp.int32)
    onehot = (train_labels[:, 0:1] == classes[None, :]).astype(jnp.float32)
    counts = jnp.sum(onehot, axis=0)
    sums = jnp.dot(onehot.T, train_rows.astype(jnp.float32), precision=lax.Precision.HIGHEST)
    means = sums / counts[:, None]
    gram = jnp.dot(train_rows.T, train_rows, preferred_element_type=jnp.float32)
    pooled_cov = (gram - jnp.dot(sums.T, means, precision=lax.Precision.HIGHEST)) / (ROWS - C)
    nblocks = D // BLK
    bands = precision.astype(jnp.float32).reshape(3, nblocks, BLK, BLK)

    def score_block(item):
        rows, labels = item
        centred = rows.astype(jnp.float32) - means[labels]
        padded = jnp.pad(centred, ((0, 0), (BLK, BLK)))
        windows = padded.reshape(rows.shape[0], nblocks + 2, BLK)
        image = jnp.zeros((rows.shape[0], nblocks, BLK), jnp.float32)
        for k in range(3):
            image = image + jnp.einsum("rmj,mij->rmi", windows[:, k:k + nblocks], bands[k], precision=lax.Precision.HIGHEST)
        image = image.reshape(rows.shape[0], D)
        score = jnp.sum(centred * image, axis=1) / D
        return image.astype(jnp.bfloat16), score

    nparts = HELD // H_DEV
    whitened, distance = lax.map(score_block, (held_rows.reshape(nparts, H_DEV, D), held_labels.reshape(nparts, H_DEV)))
    return pooled_cov, whitened.reshape(HELD, D), distance.reshape(HELD)
```

```python
import jax
import jax.numpy as jnp
from jax import lax
from jax.experimental import pallas as pl
from jax.experimental.pallas import tpu as pltpu
from jax.sharding import PartitionSpec as P

C = 256
BLK = 256
MESH = pl.DeviceIdType.MESH
F32 = jnp.float32
BF16 = jnp.bfloat16
CHUNKS = 4


def padded(cells, sides, width):
    for axis, dim in sides:
        count = lax.axis_size(axis)
        ends = count - 1
        head = lax.slice_in_dim(cells, 0, width, axis=dim)
        tail = lax.slice_in_dim(cells, cells.shape[dim] - width, cells.shape[dim], axis=dim)
        cells = jnp.concatenate(
            [
                lax.ppermute(tail, axis, [(i, (i + 1) % count) for i in range(ends)]),
                cells,
                lax.ppermute(head, axis, [((i + 1) % count, i) for i in range(ends)]),
            ],
            axis=dim,
        )
    return cells


def contract_rows(left, right):
    return lax.dot_general(
        left, right, (((0,), (0,)), ((), ())), preferred_element_type=jnp.float32
    )


def general_body(train_rows, train_labels, held_rows, held_labels, precision):
    local = train_rows.shape[1]
    full = lax.all_gather(train_rows, "feat", axis=1, tiled=True)
    width = full.shape[1]
    classes = jnp.arange(C, dtype=jnp.int32)
    onehot_train = (train_labels == classes[None, :]).astype(jnp.bfloat16)
    local_sums = contract_rows(onehot_train, full)
    local_counts = jnp.sum(onehot_train.astype(jnp.float32), axis=0)
    sums, counts = lax.psum((local_sums, local_counts), "dp")
    means = sums / counts[:, None]
    feat_index = lax.axis_index("feat")
    dp_index = lax.axis_index("dp")
    dp_count = lax.axis_size("dp")
    ncols = width // dp_count
    block = lax.psum_scatter(
        contract_rows(full, train_rows), "dp", scatter_dimension=0, tiled=True
    ).T
    sums_rows = lax.dynamic_slice_in_dim(sums, feat_index * local, local, 1)
    means_cols = lax.dynamic_slice_in_dim(means, dp_index * ncols, ncols, 1)
    correction = lax.dot_general(
        sums_rows,
        means_cols,
        (((0,), (0,)), ((), ())),
        precision=lax.Precision.HIGHEST,
        preferred_element_type=jnp.float32,
    )
    denominator = float(train_rows.shape[0] * dp_count - C)
    pooled_cov = (block - correction) / denominator
    means_local = lax.dynamic_slice_in_dim(means, feat_index * local, local, 1)
    picked = means_local[held_labels]
    centred = held_rows.astype(jnp.float32) - picked
    extended = padded(centred, (("feat", 1),), BLK)
    held_count = held_rows.shape[0]
    nlocal = local // BLK
    windows = extended.reshape(held_count, nlocal + 2, BLK)
    bands = precision.astype(jnp.float32).reshape(3, nlocal, BLK, BLK)
    image = jnp.zeros((held_count, nlocal, BLK), jnp.float32)
    for k in range(3):
        image = image + jnp.einsum(
            "rmj,mij->rmi",
            windows[:, k : k + nlocal],
            bands[k],
            precision=lax.Precision.HIGHEST,
            preferred_element_type=jnp.float32,
        )
    image = image.reshape(held_count, local)
    partial_score = jnp.sum(centred * image, axis=1)
    distance = lax.psum(partial_score, "feat") / width
    return (pooled_cov, image.astype(jnp.bfloat16), distance)


def nt(left, right):
    return lax.dot_general(left, right, (((1,), (1,)), ((), ())), preferred_element_type=F32)


def nn(left, right):
    return lax.dot_general(left, right, (((1,), (0,)), ((), ())), preferred_element_type=F32)


def split(value):
    high = value.astype(BF16)
    return high, (value - high.astype(F32)).astype(BF16)


def gather_kernel(
    train, labels, held, held_labels, prec,
    lhs, rhs, white, dist,
    tf, td, tail_l, tail_r, lab, hext, mhi, mlo, img, onehot_t, onehot_h, dacc, dsend, drecv,
    z_recv, up_send, dn_send, d_recv, sib_send, och_send,
    lab_send, lab_recv, he_send, he_recv, me_send, me_recv, ds_send, ds_recv, own_sem, out_sem,
):
    n = 4
    f = lax.axis_index("feat")
    z = lax.axis_index("dp")
    rows, local = train.shape
    nheld = held.shape[0]
    nloc = local // BLK
    cr = rows // CHUNKS
    core = lax.rem(f, 2)
    sib = f + 1 - 2 * core
    chip = f // 2
    ochip = 1 - chip
    root = f == z
    near = chip == z // 2

    def others(i):
        return [lax.rem(i + s, n) for s in range(1, n)]

    barrier = pltpu.get_barrier_semaphore()
    for o in others(z):
        pl.semaphore_signal(barrier, inc=1, device_id={"dp": o}, device_id_type=MESH)
    for o in others(f):
        pl.semaphore_signal(barrier, inc=1, device_id={"feat": o}, device_id_type=MESH)
    pl.semaphore_wait(barrier, 2 * (n - 1))

    def remote(src, dst, send, recv, where):
        return pltpu.make_async_remote_copy(
            src_ref=src, dst_ref=dst, send_sem=send, recv_sem=recv,
            device_id=where, device_id_type=MESH,
        )

    def part(c):
        return pl.ds(pl.multiple_of(c * cr, cr), cr)

    up = {"dp": jnp.minimum(z + 1, n - 1)}
    dn = {"dp": jnp.maximum(z - 1, 0)}

    def up_copy(o, c, src):
        return remote(src, tf.at[o, part(c)], up_send.at[o, c], z_recv.at[o, c], up)

    def dn_copy(o, c, src):
        return remote(src, tf.at[o, part(c)], dn_send.at[o, c], z_recv.at[o, c], dn)

    def sib_copy(o, c, src):
        return remote(src, td.at[o, part(c)], sib_send.at[o, c], d_recv.at[o, c], {"feat": sib})

    def och_copy(o, c, src):
        where = {"feat": 2 * ochip + lax.rem(c, 2)}
        return remote(src, td.at[o, part(c)], och_send.at[o, c], d_recv.at[o, c], where)

    def own_copy(o, c, src):
        return pltpu.make_async_copy(src, td.at[o, part(c)], own_sem.at[o, c])

    def send_on(o, c, src):
        @pl.when((o <= z) & (z < n - 1))
        def _():
            up_copy(o, c, src).start()

        @pl.when((o >= z) & (z > 0))
        def _():
            dn_copy(o, c, src).start()

        @pl.when(root)
        def _():
            och_copy(o, c, src).start()
            sib_copy(o, c, src).start()
            own_copy(o, c, src).start()

    def tf_event(o, c):
        src = tf.at[o, part(c)]
        up_copy(o, c, src).wait_recv()
        send_on(o, c, src)

    def td_event(o, c):
        dst = td.at[o, part(c)]

        @pl.when(root)
        def _():
            own_copy(o, c, tf.at[o, part(c)]).wait()

        @pl.when(jnp.logical_not(root))
        def _():
            sib_copy(o, c, dst).wait_recv()

        @pl.when(jnp.logical_not(near) & (lax.rem(c, 2) == core))
        def _():
            sib_copy(o, c, dst).start()

    lab_copies = [
        remote(labels, lab.at[z], lab_send.at[i], lab_recv.at[z], {"dp": o})
        for i, o in enumerate(others(z))
    ]
    for copy in lab_copies:
        copy.start()

    @pl.loop(0, CHUNKS)
    def _(c):
        send_on(z, c, train.at[part(c)])

    left = {"feat": jnp.maximum(f - 1, 0)}
    right = {"feat": jnp.minimum(f + 1, n - 1)}
    first = pl.ds(0, BLK)
    last = pl.ds(local + BLK, BLK)
    head = pl.ds(BLK, BLK)
    end = pl.ds(local, BLK)

    he_left = remote(
        held.at[:, pl.ds(0, BLK)], hext.at[:, last], he_send.at[0], he_recv.at[1], left
    )
    he_right = remote(
        held.at[:, pl.ds(local - BLK, BLK)], hext.at[:, first], he_send.at[1], he_recv.at[0], right
    )

    @pl.when(f > 0)
    def _():
        he_left.start()

    @pl.when(f < n - 1)
    def _():
        he_right.start()

    tf[z] = train[...]
    lab[z] = labels[...]
    hext[:, pl.ds(BLK, local)] = held[...]

    @pl.when(f == 0)
    def _():
        hext[:, first] = jnp.zeros((nheld, BLK), BF16)
        mhi[:, first] = jnp.zeros((C, BLK), BF16)
        mlo[:, first] = jnp.zeros((C, BLK), BF16)

    @pl.when(f == n - 1)
    def _():
        hext[:, last] = jnp.zeros((nheld, BLK), BF16)
        mhi[:, last] = jnp.zeros((C, BLK), BF16)
        mlo[:, last] = jnp.zeros((C, BLK), BF16)

    classes = lax.broadcasted_iota(jnp.int32, (C, nheld), 0)
    hot = (held_labels[0:1, :] == classes).astype(F32)
    onehot_h[...] = hot.T.astype(BF16)

    @pl.when(f > 0)
    def _():
        he_right.wait_recv()

    @pl.when(f < n - 1)
    def _():
        he_left.wait_recv()

    def block(i):
        return pl.ds(pl.multiple_of(i * BLK, BLK), BLK)

    @pl.loop(0, nloc)
    def _(m):
        total = nt(hext[:, block(m)], prec[0, block(m), :])
        for k in (1, 2):
            total += nt(hext[:, block(m + k)], prec[k, block(m), :])
        img[:, block(m)] = total

    for i, o in enumerate(others(z)):
        remote(labels, lab.at[o], lab_send.at[i], lab_recv.at[o], {"dp": o}).wait_recv()
    for o in range(n):
        ids = lax.broadcasted_iota(jnp.int32, (C, rows), 0)
        onehot_t[:, o * rows : (o + 1) * rows] = (lab[o, 0:1, :] == ids).astype(F32).astype(BF16)

    def out_copies(o):
        where = pl.ds(pl.multiple_of(o * rows, rows), rows)
        return (
            pltpu.make_async_copy(tf.at[o], lhs.at[where], out_sem.at[0, o]),
            pltpu.make_async_copy(td.at[o], rhs.at[where], out_sem.at[1, o]),
        )

    @pl.loop(0, CHUNKS)
    def _(c):
        td_event(z, c)

    for s in range(1, n):

        @pl.loop(0, CHUNKS + 1)
        def _(c, s=s):
            for o in (z - s, z + s):

                @pl.when((o >= 0) & (o < n) & (c < CHUNKS))
                def _():
                    tf_event(o, c)

            for o in (z - s, z + s):

                @pl.when((o >= 0) & (o < n) & (c > 0))
                def _():
                    td_event(o, c - 1)

    for o in range(n):
        for copy in out_copies(o):
            copy.start()

    counts = jnp.sum(onehot_t[...].astype(F32), axis=1, keepdims=True)
    inverse = 1.0 / counts

    @pl.loop(0, nloc)
    def _(m):
        total = nn(onehot_t[:, 0:rows], tf[0, :, block(m)])
        for o in range(1, n):
            total += nn(onehot_t[:, o * rows : (o + 1) * rows], tf[o, :, block(m)])
        high, low = split(total)
        tail_l[0:C, block(m)] = high
        tail_l[C : 2 * C, block(m)] = high
        tail_l[2 * C : 3 * C, block(m)] = low
        high, low = split(total * inverse)
        mhi[:, block(m + 1)] = high
        mlo[:, block(m + 1)] = low

    me_left = [
        remote(ref.at[:, head], ref.at[:, last], me_send.at[0, i], me_recv.at[1, i], left)
        for i, ref in enumerate((mhi, mlo))
    ]
    me_right = [
        remote(ref.at[:, end], ref.at[:, first], me_send.at[1, i], me_recv.at[0, i], right)
        for i, ref in enumerate((mhi, mlo))
    ]

    @pl.when(f > 0)
    def _():
        for copy in me_left:
            copy.start()

    @pl.when(f < n - 1)
    def _():
        for copy in me_right:
            copy.start()

    @pl.loop(0, nloc)
    def _(m):
        total = nn(onehot_t[:, 0:rows], td[0, :, block(m)])
        for o in range(1, n):
            total += nn(onehot_t[:, o * rows : (o + 1) * rows], td[o, :, block(m)])
        high, low = split(-(total * inverse))
        tail_r[0:C, block(m)] = high
        tail_r[C : 2 * C, block(m)] = low
        tail_r[2 * C : 3 * C, block(m)] = high

    below = pl.ds(n * rows, 3 * C)
    tail_copies = (
        pltpu.make_async_copy(tail_l, lhs.at[below], out_sem.at[0, n]),
        pltpu.make_async_copy(tail_r, rhs.at[below], out_sem.at[1, n]),
    )
    for copy in tail_copies:
        copy.start()

    @pl.when(f > 0)
    def _():
        for copy in me_right:
            copy.wait_recv()

    @pl.when(f < n - 1)
    def _():
        for copy in me_left:
            copy.wait_recv()

    dacc[...] = jnp.zeros_like(dacc)

    @pl.loop(0, nloc)
    def _(m):
        shift = jnp.zeros((C, BLK), F32)
        for k in range(3):
            band = prec[k, block(m), :]
            shift += nt(mhi[:, block(m + k)], band) + nt(mlo[:, block(m + k)], band)
        high, low = split(shift)
        pick = onehot_h[...]
        image = img[:, block(m)] - (nn(pick, high) + nn(pick, low))
        white[:, block(m)] = image.astype(BF16)
        picked = nn(pick, mhi[:, block(m + 1)]) + nn(pick, mlo[:, block(m + 1)])
        score = (held[:, block(m)].astype(F32) - picked) * image
        dacc[...] += score[:, 0:128] + score[:, 128:256]

    row = jnp.sum(dacc[...].T, axis=0, keepdims=True)
    dsend[...] = jnp.broadcast_to(row, dsend.shape)
    ds_copies = [
        remote(dsend, drecv.at[f], ds_send.at[i], ds_recv.at[f], {"feat": o})
        for i, o in enumerate(others(f))
    ]
    for copy in ds_copies:
        copy.start()
    for i, o in enumerate(others(f)):
        remote(dsend, drecv.at[o], ds_send.at[i], ds_recv.at[o], {"feat": o}).wait_recv()
    total = row
    for o in others(f):
        total += drecv[o, 0:1, :]
    dist[...] = total * (1.0 / (local * n))

    for copy in lab_copies + ds_copies:
        copy.wait_send()

    @pl.when(f > 0)
    def _():
        for copy in [he_left] + me_left:
            copy.wait_send()

    @pl.when(f < n - 1)
    def _():
        for copy in [he_right] + me_right:
            copy.wait_send()

    @pl.loop(0, n * CHUNKS)
    def _(i):
        o = i // CHUNKS
        c = lax.rem(i, CHUNKS)
        src = tf.at[o, part(c)]

        @pl.when((o <= z) & (z < n - 1))
        def _():
            up_copy(o, c, src).wait_send()

        @pl.when((o >= z) & (z > 0))
        def _():
            dn_copy(o, c, src).wait_send()

        @pl.when(root)
        def _():
            och_copy(o, c, src).wait_send()

        @pl.when(root | (jnp.logical_not(near) & (lax.rem(c, 2) == core)))
        def _():
            sib_copy(o, c, src).wait_send()

    for o in range(n):
        for copy in out_copies(o):
            copy.wait()
    for copy in tail_copies:
        copy.wait()


def square_body(train_rows, train_labels, held_rows, held_labels, precision):
    rows, local = train_rows.shape
    nheld = held_rows.shape[0]
    n = lax.axis_size("dp")
    labels = jnp.broadcast_to(train_labels.reshape(1, rows), (8, rows))
    hlabels = jnp.broadcast_to(held_labels.reshape(1, nheld), (8, nheld))
    depth = n * rows + 3 * C
    vmem = pl.BlockSpec(memory_space=pltpu.VMEM)
    hbm = pl.BlockSpec(memory_space=pl.ANY)
    dma = pltpu.SemaphoreType.DMA
    lhs, rhs, white, dist = pl.pallas_call(
        gather_kernel,
        out_shape=(
            jax.ShapeDtypeStruct((depth, local), BF16),
            jax.ShapeDtypeStruct((depth, local), BF16),
            jax.ShapeDtypeStruct((nheld, local), BF16),
            jax.ShapeDtypeStruct((1, nheld), F32),
        ),
        in_specs=[vmem] * 5,
        out_specs=(hbm, hbm, vmem, vmem),
        scratch_shapes=[
            pltpu.VMEM((n, rows, local), BF16),
            pltpu.VMEM((n, rows, local), BF16),
            pltpu.VMEM((3 * C, local), BF16),
            pltpu.VMEM((3 * C, local), BF16),
            pltpu.VMEM((n, 8, rows), jnp.int32),
            pltpu.VMEM((nheld, local + 2 * BLK), BF16),
            pltpu.VMEM((C, local + 2 * BLK), BF16),
            pltpu.VMEM((C, local + 2 * BLK), BF16),
            pltpu.VMEM((nheld, local), F32),
            pltpu.VMEM((C, n * rows), BF16),
            pltpu.VMEM((nheld, C), BF16),
            pltpu.VMEM((nheld, 128), F32),
            pltpu.VMEM((8, nheld), F32),
            pltpu.VMEM((n, 8, nheld), F32),
            dma((n, CHUNKS)),
            dma((n, CHUNKS)),
            dma((n, CHUNKS)),
            dma((n, CHUNKS)),
            dma((n, CHUNKS)),
            dma((n, CHUNKS)),
            dma((n - 1,)),
            dma((n,)),
            dma((2,)),
            dma((2,)),
            dma((2, 2)),
            dma((2, 2)),
            dma((n - 1,)),
            dma((n,)),
            dma((n, CHUNKS)),
            dma((2, n + 1)),
        ],
        compiler_params=pltpu.CompilerParams(
            collective_id=0, has_side_effects=True, vmem_limit_bytes=40 * 1024 * 1024
        ),
    )(train_rows, labels, held_rows, hlabels, precision)
    pooled_cov = contract_rows(lhs, rhs) * (1.0 / float(rows * n - C))
    return pooled_cov, white, dist.reshape(nheld)


def solution(mesh):
    square = mesh.shape["dp"] == 4 and mesh.shape["feat"] == 4
    return jax.shard_map(
        square_body if square else general_body,
        mesh=mesh,
        in_specs=(
            P(("layer", "dp"), "feat"),
            P(("layer", "dp"), None),
            P(("layer", "dp"), "feat"),
            P(("layer", "dp")),
            P("layer", "feat", None),
        ),
        out_specs=(P(("layer", "feat"), "dp"), P(("layer", "dp"), "feat"), P(("layer", "dp"))),
        check_vma=False,
    )
```

```python
import jax
import jax.numpy as jnp
from jax import lax
from jax.experimental import pallas as pl
from jax.experimental.pallas import tpu as pltpu
from jax.sharding import PartitionSpec as P

C = 256
BLK = 256
MESH = pl.DeviceIdType.MESH
F32 = jnp.float32
BF16 = jnp.bfloat16
CHUNKS = 4


def padded(cells, sides, width):
    for axis, dim in sides:
        count = lax.axis_size(axis)
        ends = count - 1
        head = lax.slice_in_dim(cells, 0, width, axis=dim)
        tail = lax.slice_in_dim(cells, cells.shape[dim] - width, cells.shape[dim], axis=dim)
        cells = jnp.concatenate(
            [
                lax.ppermute(tail, axis, [(i, (i + 1) % count) for i in range(ends)]),
                cells,
                lax.ppermute(head, axis, [((i + 1) % count, i) for i in range(ends)]),
            ],
            axis=dim,
        )
    return cells


def contract_rows(left, right):
    return lax.dot_general(
        left, right, (((0,), (0,)), ((), ())), preferred_element_type=jnp.float32
    )


def general_body(train_rows, train_labels, held_rows, held_labels, precision):
    local = train_rows.shape[1]
    full = lax.all_gather(train_rows, "feat", axis=1, tiled=True)
    width = full.shape[1]
    classes = jnp.arange(C, dtype=jnp.int32)
    onehot_train = (train_labels == classes[None, :]).astype(jnp.bfloat16)
    local_sums = contract_rows(onehot_train, full)
    local_counts = jnp.sum(onehot_train.astype(jnp.float32), axis=0)
    sums, counts = lax.psum((local_sums, local_counts), "dp")
    means = sums / counts[:, None]
    feat_index = lax.axis_index("feat")
    dp_index = lax.axis_index("dp")
    dp_count = lax.axis_size("dp")
    ncols = width // dp_count
    block = lax.psum_scatter(
        contract_rows(full, train_rows), "dp", scatter_dimension=0, tiled=True
    ).T
    sums_rows = lax.dynamic_slice_in_dim(sums, feat_index * local, local, 1)
    means_cols = lax.dynamic_slice_in_dim(means, dp_index * ncols, ncols, 1)
    correction = lax.dot_general(
        sums_rows,
        means_cols,
        (((0,), (0,)), ((), ())),
        precision=lax.Precision.HIGHEST,
        preferred_element_type=jnp.float32,
    )
    denominator = float(train_rows.shape[0] * dp_count - C)
    pooled_cov = (block - correction) / denominator
    means_local = lax.dynamic_slice_in_dim(means, feat_index * local, local, 1)
    picked = means_local[held_labels]
    centred = held_rows.astype(jnp.float32) - picked
    extended = padded(centred, (("feat", 1),), BLK)
    held_count = held_rows.shape[0]
    nlocal = local // BLK
    windows = extended.reshape(held_count, nlocal + 2, BLK)
    bands = precision.astype(jnp.float32).reshape(3, nlocal, BLK, BLK)
    image = jnp.zeros((held_count, nlocal, BLK), jnp.float32)
    for k in range(3):
        image = image + jnp.einsum(
            "rmj,mij->rmi",
            windows[:, k : k + nlocal],
            bands[k],
            precision=lax.Precision.HIGHEST,
            preferred_element_type=jnp.float32,
        )
    image = image.reshape(held_count, local)
    partial_score = jnp.sum(centred * image, axis=1)
    distance = lax.psum(partial_score, "feat") / width
    return (pooled_cov, image.astype(jnp.bfloat16), distance)


def nt(left, right):
    return lax.dot_general(left, right, (((1,), (1,)), ((), ())), preferred_element_type=F32)


def nn(left, right):
    return lax.dot_general(left, right, (((1,), (0,)), ((), ())), preferred_element_type=F32)


def split(value):
    high = value.astype(BF16)
    return high, (value - high.astype(F32)).astype(BF16)


def gather_kernel(
    train_hbm, labels, held_hbm, held_labels, prec_hbm,
    cov, white, dist,
    train, prec, tf, td, sf, sd, tail_l, tail_r, lab, hext, mhi, mlo, img, onehot_t, onehot_h,
    dacc, dsend, drecv,
    z_recv, up_send, dn_send, d_recv, sib_send, och_send,
    lab_send, lab_recv, he_send, he_recv, me_send, me_recv, ds_send, ds_recv, own_sem, in_sem,
):
    n = 4
    f = lax.axis_index("feat")
    z = lax.axis_index("dp")
    rows, local = train.shape
    nheld = held_hbm.shape[0]
    nloc = local // BLK
    cr = rows // CHUNKS
    core = lax.rem(f, 2)
    sib = f + 1 - 2 * core
    chip = f // 2
    ochip = 1 - chip
    root = f == z
    near = chip == z // 2

    def others(i):
        return [lax.rem(i + s, n) for s in range(1, n)]

    train_in = pltpu.make_async_copy(train_hbm, train, in_sem.at[0])
    held_in = pltpu.make_async_copy(held_hbm, hext.at[:, pl.ds(BLK, local)], in_sem.at[1])
    prec_in = pltpu.make_async_copy(prec_hbm, prec, in_sem.at[2])
    for copy in (train_in, held_in, prec_in):
        copy.start()

    barrier = pltpu.get_barrier_semaphore()
    for o in others(z):
        pl.semaphore_signal(barrier, inc=1, device_id={"dp": o}, device_id_type=MESH)
    for o in others(f):
        pl.semaphore_signal(barrier, inc=1, device_id={"feat": o}, device_id_type=MESH)
    pl.semaphore_wait(barrier, 2 * (n - 1))

    def remote(src, dst, send, recv, where):
        return pltpu.make_async_remote_copy(
            src_ref=src, dst_ref=dst, send_sem=send, recv_sem=recv,
            device_id=where, device_id_type=MESH,
        )

    def part(c):
        return pl.ds(pl.multiple_of(c * cr, cr), cr)

    up = {"dp": jnp.minimum(z + 1, n - 1)}
    dn = {"dp": jnp.maximum(z - 1, 0)}

    def up_copy(o, c, src):
        return remote(src, tf.at[o, part(c)], up_send.at[o, c], z_recv.at[o, c], up)

    def dn_copy(o, c, src):
        return remote(src, tf.at[o, part(c)], dn_send.at[o, c], z_recv.at[o, c], dn)

    def sib_copy(o, c, src):
        return remote(src, td.at[o, part(c)], sib_send.at[o, c], d_recv.at[o, c], {"feat": sib})

    def och_copy(o, c, src):
        where = {"feat": 2 * ochip + lax.rem(c, 2)}
        return remote(src, td.at[o, part(c)], och_send.at[o, c], d_recv.at[o, c], where)

    def own_copy(o, c, src):
        return pltpu.make_async_copy(src, td.at[o, part(c)], own_sem.at[o, c])

    def send_on(o, c, src):
        @pl.when((o <= z) & (z < n - 1))
        def _():
            up_copy(o, c, src).start()

        @pl.when((o >= z) & (z > 0))
        def _():
            dn_copy(o, c, src).start()

        @pl.when(root)
        def _():
            och_copy(o, c, src).start()
            sib_copy(o, c, src).start()
            own_copy(o, c, src).start()

    def tf_event(o, c):
        src = tf.at[o, part(c)]
        up_copy(o, c, src).wait_recv()
        send_on(o, c, src)

    def td_event(o, c):
        dst = td.at[o, part(c)]

        @pl.when(root)
        def _():
            own_copy(o, c, tf.at[o, part(c)]).wait()

        @pl.when(jnp.logical_not(root))
        def _():
            sib_copy(o, c, dst).wait_recv()

        @pl.when(jnp.logical_not(near) & (lax.rem(c, 2) == core))
        def _():
            sib_copy(o, c, dst).start()

    lab[z] = jnp.broadcast_to(labels[...], lab.shape[1:])

    lab_copies = [
        remote(lab.at[z], lab.at[z], lab_send.at[i], lab_recv.at[z], {"dp": o})
        for i, o in enumerate(others(z))
    ]
    for copy in lab_copies:
        copy.start()

    train_in.wait()

    @pl.loop(0, CHUNKS)
    def _(c):
        send_on(z, c, train.at[part(c)])

    left = {"feat": jnp.maximum(f - 1, 0)}
    right = {"feat": jnp.minimum(f + 1, n - 1)}
    first = pl.ds(0, BLK)
    last = pl.ds(local + BLK, BLK)
    head = pl.ds(BLK, BLK)
    end = pl.ds(local, BLK)

    he_left = remote(
        hext.at[:, head], hext.at[:, last], he_send.at[0], he_recv.at[1], left
    )
    he_right = remote(
        hext.at[:, end], hext.at[:, first], he_send.at[1], he_recv.at[0], right
    )

    held_in.wait()

    @pl.when(f > 0)
    def _():
        he_left.start()

    @pl.when(f < n - 1)
    def _():
        he_right.start()

    tf[z] = train[...]

    @pl.when(f == 0)
    def _():
        hext[:, first] = jnp.zeros((nheld, BLK), BF16)
        mhi[:, first] = jnp.zeros((C, BLK), BF16)
        mlo[:, first] = jnp.zeros((C, BLK), BF16)

    @pl.when(f == n - 1)
    def _():
        hext[:, last] = jnp.zeros((nheld, BLK), BF16)
        mhi[:, last] = jnp.zeros((C, BLK), BF16)
        mlo[:, last] = jnp.zeros((C, BLK), BF16)

    classes = lax.broadcasted_iota(jnp.int32, (C, nheld), 0)
    hot = (held_labels[0:1, :] == classes).astype(F32)
    onehot_h[...] = hot.T.astype(BF16)

    @pl.when(f > 0)
    def _():
        he_right.wait_recv()

    @pl.when(f < n - 1)
    def _():
        he_left.wait_recv()

    def block(i):
        return pl.ds(pl.multiple_of(i * BLK, BLK), BLK)

    for i, o in enumerate(others(z)):
        remote(lab.at[o], lab.at[o], lab_send.at[i], lab_recv.at[o], {"dp": o}).wait_recv()
    counts = jnp.zeros((C, 1), F32)
    for o in range(n):
        ids = lax.broadcasted_iota(jnp.int32, (C, rows), 0)
        hot = (lab[o, 0:1, :] == ids).astype(F32)
        onehot_t[o] = hot.astype(BF16)
        counts += jnp.sum(hot, axis=1, keepdims=True)
    inverse = 1.0 / counts
    prec_in.wait()

    @pl.loop(0, nloc)
    def _(m):
        total = nt(hext[:, block(m)], prec[0, block(m), :])
        for k in (1, 2):
            total += nt(hext[:, block(m + k)], prec[k, block(m), :])
        img[:, block(m)] = total

    @pl.loop(0, CHUNKS)
    def _(c):
        td_event(z, c)

    def absorb_f(o, m):
        sf[:, block(m)] += nn(onehot_t[o], tf[o, :, block(m)])

    def absorb_d(o, m):
        sd[:, block(m)] += nn(onehot_t[o], td[o, :, block(m)])
        cov[block(m), :] += contract_rows(tf[o, :, block(m)], td[o])

    def first_piece(m):
        sf[:, block(m)] = nn(onehot_t[z], tf[z, :, block(m)])
        sd[:, block(m)] = nn(onehot_t[z], td[z, :, block(m)])
        cov[block(m), :] = contract_rows(tf[z, :, block(m)], td[z])

    for s in range(1, n):

        @pl.loop(0, CHUNKS)
        def _(c, s=s):
            for o in (z - s, z + s):

                @pl.when((o >= 0) & (o < n))
                def _():
                    tf_event(o, c)

            for o in (z - s, z + s):

                @pl.when((o >= 0) & (o < n) & (c > 0))
                def _():
                    td_event(o, c - 1)

            if s == 1:
                first_piece(c)
            else:
                for o in (z - s + 1, z + s - 1):

                    @pl.when((o >= 0) & (o < n))
                    def _():
                        absorb_f(o, c)
                        absorb_d(o, c)

        if s < n - 1:
            for o in (z - s, z + s):

                @pl.when((o >= 0) & (o < n))
                def _():
                    td_event(o, CHUNKS - 1)

    for o in (z - n + 1, z + n - 1):

        @pl.when((o >= 0) & (o < n))
        def _():
            @pl.loop(0, nloc)
            def _(m):
                absorb_f(o, m)

    @pl.loop(0, nloc)
    def _(m):
        total = sf[:, block(m)]
        high, low = split(total)
        tail_l[0:C, block(m)] = high
        tail_l[C : 2 * C, block(m)] = high
        tail_l[2 * C : 3 * C, block(m)] = low
        high, low = split(total * inverse)
        mhi[:, block(m + 1)] = high
        mlo[:, block(m + 1)] = low

    me_left = [
        remote(ref.at[:, head], ref.at[:, last], me_send.at[0, i], me_recv.at[1, i], left)
        for i, ref in enumerate((mhi, mlo))
    ]
    me_right = [
        remote(ref.at[:, end], ref.at[:, first], me_send.at[1, i], me_recv.at[0, i], right)
        for i, ref in enumerate((mhi, mlo))
    ]

    @pl.when(f > 0)
    def _():
        for copy in me_left:
            copy.start()

    @pl.when(f < n - 1)
    def _():
        for copy in me_right:
            copy.start()

    for o in (z - n + 1, z + n - 1):

        @pl.when((o >= 0) & (o < n))
        def _():
            td_event(o, CHUNKS - 1)

            @pl.loop(0, nloc)
            def _(m):
                absorb_d(o, m)

    @pl.loop(0, nloc)
    def _(m):
        high, low = split(-(sd[:, block(m)] * inverse))
        tail_r[0:C, block(m)] = high
        tail_r[C : 2 * C, block(m)] = low
        tail_r[2 * C : 3 * C, block(m)] = high

    scale = 1.0 / float(rows * n - C)

    def finish(m):
        total = cov[block(m), :] + contract_rows(tail_l[:, block(m)], tail_r[...])
        cov[block(m), :] = total * scale

    @pl.loop(0, nloc // 2)
    def _(m):
        finish(m)

    @pl.when(f > 0)
    def _():
        for copy in me_right:
            copy.wait_recv()

    @pl.when(f < n - 1)
    def _():
        for copy in me_left:
            copy.wait_recv()

    dacc[...] = jnp.zeros_like(dacc)

    @pl.loop(0, nloc)
    def _(m):
        shift = jnp.zeros((C, BLK), F32)
        for k in range(3):
            band = prec[k, block(m), :]
            shift += nt(mhi[:, block(m + k)], band) + nt(mlo[:, block(m + k)], band)
        high, low = split(shift)
        pick = onehot_h[...]
        image = img[:, block(m)] - (nn(pick, high) + nn(pick, low))
        white[:, block(m)] = image.astype(BF16)
        picked = nn(pick, mhi[:, block(m + 1)]) + nn(pick, mlo[:, block(m + 1)])
        score = (hext[:, block(m + 1)].astype(F32) - picked) * image
        dacc[...] += score[:, 0:128] + score[:, 128:256]

    row = jnp.sum(dacc[...].T, axis=0, keepdims=True)
    dsend[...] = jnp.broadcast_to(row, dsend.shape)
    ds_copies = [
        remote(dsend, drecv.at[f], ds_send.at[i], ds_recv.at[f], {"feat": o})
        for i, o in enumerate(others(f))
    ]
    for copy in ds_copies:
        copy.start()

    @pl.loop(nloc // 2, nloc)
    def _(m):
        finish(m)

    for i, o in enumerate(others(f)):
        remote(dsend, drecv.at[o], ds_send.at[i], ds_recv.at[o], {"feat": o}).wait_recv()
    total = row
    for o in others(f):
        total += drecv[o, 0:1, :]
    dist[...] = total * (1.0 / (local * n))

    for copy in lab_copies + ds_copies:
        copy.wait_send()

    @pl.when(f > 0)
    def _():
        for copy in [he_left] + me_left:
            copy.wait_send()

    @pl.when(f < n - 1)
    def _():
        for copy in [he_right] + me_right:
            copy.wait_send()

    @pl.loop(0, n * CHUNKS)
    def _(i):
        o = i // CHUNKS
        c = lax.rem(i, CHUNKS)
        src = tf.at[o, part(c)]

        @pl.when((o <= z) & (z < n - 1))
        def _():
            up_copy(o, c, src).wait_send()

        @pl.when((o >= z) & (z > 0))
        def _():
            dn_copy(o, c, src).wait_send()

        @pl.when(root)
        def _():
            och_copy(o, c, src).wait_send()

        @pl.when(root | (jnp.logical_not(near) & (lax.rem(c, 2) == core)))
        def _():
            sib_copy(o, c, src).wait_send()


def square_body(train_rows, train_labels, held_rows, held_labels, precision):
    rows, local = train_rows.shape
    nheld = held_rows.shape[0]
    n = lax.axis_size("dp")
    labels = train_labels.reshape(1, rows)
    hlabels = held_labels.reshape(1, nheld)
    vmem = pl.BlockSpec(memory_space=pltpu.VMEM)
    hbm = pl.BlockSpec(memory_space=pltpu.HBM)
    dma = pltpu.SemaphoreType.DMA
    cov, white, dist = pl.pallas_call(
        gather_kernel,
        out_shape=(
            jax.ShapeDtypeStruct((local, local), F32),
            jax.ShapeDtypeStruct((nheld, local), BF16),
            jax.ShapeDtypeStruct((1, nheld), F32),
        ),
        in_specs=[hbm, vmem, hbm, vmem, hbm],
        out_specs=(vmem, vmem, vmem),
        scratch_shapes=[
            pltpu.VMEM((rows, local), BF16),
            pltpu.VMEM(precision.shape, BF16),
            pltpu.VMEM((n, rows, local), BF16),
            pltpu.VMEM((n, rows, local), BF16),
            pltpu.VMEM((C, local), F32),
            pltpu.VMEM((C, local), F32),
            pltpu.VMEM((3 * C, local), BF16),
            pltpu.VMEM((3 * C, local), BF16),
            pltpu.VMEM((n, 8, rows), jnp.int32),
            pltpu.VMEM((nheld, local + 2 * BLK), BF16),
            pltpu.VMEM((C, local + 2 * BLK), BF16),
            pltpu.VMEM((C, local + 2 * BLK), BF16),
            pltpu.VMEM((nheld, local), F32),
            pltpu.VMEM((n, C, rows), BF16),
            pltpu.VMEM((nheld, C), BF16),
            pltpu.VMEM((nheld, 128), F32),
            pltpu.VMEM((8, nheld), F32),
            pltpu.VMEM((n, 8, nheld), F32),
            dma((n, CHUNKS)),
            dma((n, CHUNKS)),
            dma((n, CHUNKS)),
            dma((n, CHUNKS)),
            dma((n, CHUNKS)),
            dma((n, CHUNKS)),
            dma((n - 1,)),
            dma((n,)),
            dma((2,)),
            dma((2,)),
            dma((2, 2)),
            dma((2, 2)),
            dma((n - 1,)),
            dma((n,)),
            dma((n, CHUNKS)),
            dma((3,)),
        ],
        compiler_params=pltpu.CompilerParams(
            collective_id=0, has_side_effects=True, vmem_limit_bytes=40 * 1024 * 1024
        ),
    )(train_rows, labels, held_rows, hlabels, precision)
    return cov, white, dist.reshape(nheld)


def solution(mesh):
    square = mesh.shape["dp"] == 4 and mesh.shape["feat"] == 4
    return jax.shard_map(
        square_body if square else general_body,
        mesh=mesh,
        in_specs=(
            P(("layer", "dp"), "feat"),
            P(("layer", "dp"), None),
            P(("layer", "dp"), "feat"),
            P(("layer", "dp")),
            P("layer", "feat", None),
        ),
        out_specs=(P(("layer", "feat"), "dp"), P(("layer", "dp"), "feat"), P(("layer", "dp"))),
        check_vma=False,
    )
```

```python
import jax
import jax.numpy as jnp
from jax import lax
from jax.experimental import pallas as pl
from jax.experimental.pallas import tpu as pltpu
from jax.sharding import PartitionSpec as P

C = 256
BLK = 256
MESH = pl.DeviceIdType.MESH
F32 = jnp.float32
BF16 = jnp.bfloat16
CHUNKS = 4


def padded(cells, sides, width):
    for axis, dim in sides:
        count = lax.axis_size(axis)
        ends = count - 1
        head = lax.slice_in_dim(cells, 0, width, axis=dim)
        tail = lax.slice_in_dim(cells, cells.shape[dim] - width, cells.shape[dim], axis=dim)
        cells = jnp.concatenate(
            [
                lax.ppermute(tail, axis, [(i, (i + 1) % count) for i in range(ends)]),
                cells,
                lax.ppermute(head, axis, [((i + 1) % count, i) for i in range(ends)]),
            ],
            axis=dim,
        )
    return cells


def contract_rows(left, right):
    return lax.dot_general(
        left, right, (((0,), (0,)), ((), ())), preferred_element_type=jnp.float32
    )


def general_body(train_rows, train_labels, held_rows, held_labels, precision):
    local = train_rows.shape[1]
    full = lax.all_gather(train_rows, "feat", axis=1, tiled=True)
    width = full.shape[1]
    classes = jnp.arange(C, dtype=jnp.int32)
    onehot_train = (train_labels == classes[None, :]).astype(jnp.bfloat16)
    local_sums = contract_rows(onehot_train, full)
    local_counts = jnp.sum(onehot_train.astype(jnp.float32), axis=0)
    sums, counts = lax.psum((local_sums, local_counts), "dp")
    means = sums / counts[:, None]
    feat_index = lax.axis_index("feat")
    dp_index = lax.axis_index("dp")
    dp_count = lax.axis_size("dp")
    ncols = width // dp_count
    block = lax.psum_scatter(
        contract_rows(full, train_rows), "dp", scatter_dimension=0, tiled=True
    ).T
    sums_rows = lax.dynamic_slice_in_dim(sums, feat_index * local, local, 1)
    means_cols = lax.dynamic_slice_in_dim(means, dp_index * ncols, ncols, 1)
    correction = lax.dot_general(
        sums_rows,
        means_cols,
        (((0,), (0,)), ((), ())),
        precision=lax.Precision.HIGHEST,
        preferred_element_type=jnp.float32,
    )
    denominator = float(train_rows.shape[0] * dp_count - C)
    pooled_cov = (block - correction) / denominator
    means_local = lax.dynamic_slice_in_dim(means, feat_index * local, local, 1)
    picked = means_local[held_labels]
    centred = held_rows.astype(jnp.float32) - picked
    extended = padded(centred, (("feat", 1),), BLK)
    held_count = held_rows.shape[0]
    nlocal = local // BLK
    windows = extended.reshape(held_count, nlocal + 2, BLK)
    bands = precision.astype(jnp.float32).reshape(3, nlocal, BLK, BLK)
    image = jnp.zeros((held_count, nlocal, BLK), jnp.float32)
    for k in range(3):
        image = image + jnp.einsum(
            "rmj,mij->rmi",
            windows[:, k : k + nlocal],
            bands[k],
            precision=lax.Precision.HIGHEST,
            preferred_element_type=jnp.float32,
        )
    image = image.reshape(held_count, local)
    partial_score = jnp.sum(centred * image, axis=1)
    distance = lax.psum(partial_score, "feat") / width
    return (pooled_cov, image.astype(jnp.bfloat16), distance)


def nt(left, right):
    return lax.dot_general(left, right, (((1,), (1,)), ((), ())), preferred_element_type=F32)


def nn(left, right):
    return lax.dot_general(left, right, (((1,), (0,)), ((), ())), preferred_element_type=F32)


def split(value):
    high = value.astype(BF16)
    return high, (value - high.astype(F32)).astype(BF16)


def gather_kernel(
    train_hbm, labels, held_hbm, held_labels, prec_hbm,
    cov, white, dist,
    train, prec, tf, td, sf, sd, tail_l, tail_r, lab, hext, mhi, mlo, img, onehot_t, onehot_h,
    dacc, dsend, drecv,
    z_recv, up_send, dn_send, d_recv, sib_send, och_send,
    lab_send, lab_recv, he_send, he_recv, me_send, me_recv, ds_send, ds_recv, own_sem, in_sem,
):
    n = 4
    f = lax.axis_index("feat")
    z = lax.axis_index("dp")
    rows, local = train.shape
    nheld = held_hbm.shape[0]
    nloc = local // BLK
    cr = rows // CHUNKS
    core = lax.rem(f, 2)
    sib = f + 1 - 2 * core
    chip = f // 2
    ochip = 1 - chip
    root = f == z
    near = chip == z // 2
    at_end = (z == 0) | (z == n - 1)

    def others(i):
        return [lax.rem(i + s, n) for s in range(1, n)]

    train_in = pltpu.make_async_copy(train_hbm, train, in_sem.at[0])
    held_in = pltpu.make_async_copy(held_hbm, hext.at[:, pl.ds(BLK, local)], in_sem.at[1])
    prec_in = pltpu.make_async_copy(prec_hbm, prec, in_sem.at[2])
    for copy in (train_in, held_in, prec_in):
        copy.start()

    barrier = pltpu.get_barrier_semaphore()
    for o in others(z):
        pl.semaphore_signal(barrier, inc=1, device_id={"dp": o}, device_id_type=MESH)
    for o in others(f):
        pl.semaphore_signal(barrier, inc=1, device_id={"feat": o}, device_id_type=MESH)
    pl.semaphore_wait(barrier, 2 * (n - 1))

    def remote(src, dst, send, recv, where):
        return pltpu.make_async_remote_copy(
            src_ref=src, dst_ref=dst, send_sem=send, recv_sem=recv,
            device_id=where, device_id_type=MESH,
        )

    def part(c):
        return pl.ds(pl.multiple_of(c * cr, cr), cr)

    up = {"dp": jnp.minimum(z + 1, n - 1)}
    dn = {"dp": jnp.maximum(z - 1, 0)}

    def up_copy(o, c, src):
        return remote(src, tf.at[o, part(c)], up_send.at[o, c], z_recv.at[o, c], up)

    def dn_copy(o, c, src):
        return remote(src, tf.at[o, part(c)], dn_send.at[o, c], z_recv.at[o, c], dn)

    def sib_copy(o, c, src):
        return remote(src, td.at[o, part(c)], sib_send.at[o, c], d_recv.at[o, c], {"feat": sib})

    def och_copy(o, c, src):
        where = {"feat": 2 * ochip + lax.rem(c, 2)}
        return remote(src, td.at[o, part(c)], och_send.at[o, c], d_recv.at[o, c], where)

    def own_copy(o, c, src):
        return pltpu.make_async_copy(src, td.at[o, part(c)], own_sem.at[o, c])

    def send_on(o, c, src):
        @pl.when((o <= z) & (z < n - 1))
        def _():
            up_copy(o, c, src).start()

        @pl.when((o >= z) & (z > 0))
        def _():
            dn_copy(o, c, src).start()

        @pl.when(root)
        def _():
            sib_copy(o, c, src).start()
            och_copy(o, c, src).start()
            own_copy(o, c, src).start()

    def tf_event(o, c):
        src = tf.at[o, part(c)]
        up_copy(o, c, src).wait_recv()
        send_on(o, c, src)

    def td_event(o, c):
        dst = td.at[o, part(c)]

        @pl.when(root)
        def _():
            own_copy(o, c, tf.at[o, part(c)]).wait()

        @pl.when(jnp.logical_not(root))
        def _():
            sib_copy(o, c, dst).wait_recv()

        @pl.when(jnp.logical_not(near) & (lax.rem(c, 2) == core))
        def _():
            sib_copy(o, c, dst).start()

    lab[z] = jnp.broadcast_to(labels[...], lab.shape[1:])

    lab_copies = [
        remote(lab.at[z], lab.at[z], lab_send.at[i], lab_recv.at[z], {"dp": o})
        for i, o in enumerate(others(z))
    ]
    for copy in lab_copies:
        copy.start()

    train_in.wait()

    @pl.loop(0, CHUNKS)
    def _(c):
        send_on(z, c, train.at[part(c)])

    left = {"feat": jnp.maximum(f - 1, 0)}
    right = {"feat": jnp.minimum(f + 1, n - 1)}
    first = pl.ds(0, BLK)
    last = pl.ds(local + BLK, BLK)
    head = pl.ds(BLK, BLK)
    end = pl.ds(local, BLK)

    he_left = remote(
        hext.at[:, head], hext.at[:, last], he_send.at[0], he_recv.at[1], left
    )
    he_right = remote(
        hext.at[:, end], hext.at[:, first], he_send.at[1], he_recv.at[0], right
    )

    held_in.wait()

    @pl.when(f > 0)
    def _():
        he_left.start()

    @pl.when(f < n - 1)
    def _():
        he_right.start()

    tf[z] = train[...]

    @pl.when(f == 0)
    def _():
        hext[:, first] = jnp.zeros((nheld, BLK), BF16)
        mhi[:, first] = jnp.zeros((C, BLK), BF16)
        mlo[:, first] = jnp.zeros((C, BLK), BF16)

    @pl.when(f == n - 1)
    def _():
        hext[:, last] = jnp.zeros((nheld, BLK), BF16)
        mhi[:, last] = jnp.zeros((C, BLK), BF16)
        mlo[:, last] = jnp.zeros((C, BLK), BF16)

    classes = lax.broadcasted_iota(jnp.int32, (C, nheld), 0)
    hot = (held_labels[0:1, :] == classes).astype(F32)
    onehot_h[...] = hot.T.astype(BF16)

    @pl.when(f > 0)
    def _():
        he_right.wait_recv()

    @pl.when(f < n - 1)
    def _():
        he_left.wait_recv()

    def block(i):
        return pl.ds(pl.multiple_of(i * BLK, BLK), BLK)

    for i, o in enumerate(others(z)):
        remote(lab.at[o], lab.at[o], lab_send.at[i], lab_recv.at[o], {"dp": o}).wait_recv()
    counts = jnp.zeros((C, 1), F32)
    for o in range(n):
        ids = lax.broadcasted_iota(jnp.int32, (C, rows), 0)
        hot = (lab[o, 0:1, :] == ids).astype(F32)
        onehot_t[o] = hot.astype(BF16)
        counts += jnp.sum(hot, axis=1, keepdims=True)
    inverse = 1.0 / counts
    prec_in.wait()

    @pl.loop(0, nloc)
    def _(m):
        total = nt(hext[:, block(m)], prec[0, block(m), :])
        for k in (1, 2):
            total += nt(hext[:, block(m + k)], prec[k, block(m), :])
        img[:, block(m)] = total

    @pl.loop(0, CHUNKS)
    def _(c):
        td_event(z, c)

    def absorb_f(o, m):
        sf[:, block(m)] += nn(onehot_t[o], tf[o, :, block(m)])

    def absorb_d(o, m):
        sd[:, block(m)] += nn(onehot_t[o], td[o, :, block(m)])
        cov[block(m), :] += contract_rows(tf[o, :, block(m)], td[o])

    def first_piece(m):
        sf[:, block(m)] = nn(onehot_t[z], tf[z, :, block(m)])
        sd[:, block(m)] = nn(onehot_t[z], td[z, :, block(m)])
        cov[block(m), :] = contract_rows(tf[z, :, block(m)], td[z])

    for s in range(1, n):

        @pl.loop(0, CHUNKS)
        def _(c, s=s):
            for o in (z - s, z + s):

                @pl.when((o >= 0) & (o < n))
                def _():
                    tf_event(o, c)

            for o in (z - s, z + s):

                @pl.when((o >= 0) & (o < n) & (c > 0))
                def _():
                    td_event(o, c - 1)

            if s == 1:
                first_piece(c)
            for t in range(1, s):
                for o in (z - t, z + t):
                    ready = (o >= 0) & (o < n)
                    if s < n - 1:
                        ready = ready & at_end & (t == s - 1)
                    elif t < s - 1:
                        ready = ready & jnp.logical_not(at_end)

                    @pl.when(ready)
                    def _():
                        absorb_f(o, c)
                        absorb_d(o, c)

        if s < n - 1:
            for o in (z - s, z + s):

                @pl.when((o >= 0) & (o < n))
                def _():
                    td_event(o, CHUNKS - 1)

    for o in (z - n + 1, z + n - 1):

        @pl.when((o >= 0) & (o < n))
        def _():
            @pl.loop(0, nloc)
            def _(m):
                absorb_f(o, m)

    @pl.loop(0, nloc)
    def _(m):
        total = sf[:, block(m)]
        high, low = split(total)
        tail_l[0:C, block(m)] = high
        tail_l[C : 2 * C, block(m)] = high
        tail_l[2 * C : 3 * C, block(m)] = low
        high, low = split(total * inverse)
        mhi[:, block(m + 1)] = high
        mlo[:, block(m + 1)] = low

    me_left = [
        remote(ref.at[:, head], ref.at[:, last], me_send.at[0, i], me_recv.at[1, i], left)
        for i, ref in enumerate((mhi, mlo))
    ]
    me_right = [
        remote(ref.at[:, end], ref.at[:, first], me_send.at[1, i], me_recv.at[0, i], right)
        for i, ref in enumerate((mhi, mlo))
    ]

    @pl.when(f > 0)
    def _():
        for copy in me_left:
            copy.start()

    @pl.when(f < n - 1)
    def _():
        for copy in me_right:
            copy.start()

    for o in (z - n + 1, z + n - 1):

        @pl.when((o >= 0) & (o < n))
        def _():
            td_event(o, CHUNKS - 1)

            @pl.loop(0, nloc)
            def _(m):
                absorb_d(o, m)

    @pl.when(f > 0)
    def _():
        for copy in me_right:
            copy.wait_recv()

    @pl.when(f < n - 1)
    def _():
        for copy in me_left:
            copy.wait_recv()

    dacc[...] = jnp.zeros_like(dacc)

    @pl.loop(0, nloc)
    def _(m):
        shift = jnp.zeros((C, BLK), F32)
        for k in range(3):
            band = prec[k, block(m), :]
            shift += nt(mhi[:, block(m + k)], band) + nt(mlo[:, block(m + k)], band)
        high, low = split(shift)
        pick = onehot_h[...]
        image = img[:, block(m)] - (nn(pick, high) + nn(pick, low))
        white[:, block(m)] = image.astype(BF16)
        picked = nn(pick, mhi[:, block(m + 1)]) + nn(pick, mlo[:, block(m + 1)])
        score = (hext[:, block(m + 1)].astype(F32) - picked) * image
        dacc[...] += score[:, 0:128] + score[:, 128:256]

    row = jnp.sum(dacc[...].T, axis=0, keepdims=True)
    dsend[...] = jnp.broadcast_to(row, dsend.shape)
    ds_copies = [
        remote(dsend, drecv.at[f], ds_send.at[i], ds_recv.at[f], {"feat": o})
        for i, o in enumerate(others(f))
    ]
    for copy in ds_copies:
        copy.start()

    @pl.loop(0, nloc)
    def _(m):
        high, low = split(-(sd[:, block(m)] * inverse))
        tail_r[0:C, block(m)] = high
        tail_r[C : 2 * C, block(m)] = low
        tail_r[2 * C : 3 * C, block(m)] = high

    scale = 1.0 / float(rows * n - C)

    @pl.loop(0, nloc)
    def _(m):
        total = cov[block(m), :] + contract_rows(tail_l[:, block(m)], tail_r[...])
        cov[block(m), :] = total * scale

    for i, o in enumerate(others(f)):
        remote(dsend, drecv.at[o], ds_send.at[i], ds_recv.at[o], {"feat": o}).wait_recv()
    total = row
    for o in others(f):
        total += drecv[o, 0:1, :]
    dist[...] = total * (1.0 / (local * n))

    for copy in lab_copies + ds_copies:
        copy.wait_send()

    @pl.when(f > 0)
    def _():
        for copy in [he_left] + me_left:
            copy.wait_send()

    @pl.when(f < n - 1)
    def _():
        for copy in [he_right] + me_right:
            copy.wait_send()

    @pl.loop(0, n * CHUNKS)
    def _(i):
        o = i // CHUNKS
        c = lax.rem(i, CHUNKS)
        src = tf.at[o, part(c)]

        @pl.when((o <= z) & (z < n - 1))
        def _():
            up_copy(o, c, src).wait_send()

        @pl.when((o >= z) & (z > 0))
        def _():
            dn_copy(o, c, src).wait_send()

        @pl.when(root)
        def _():
            och_copy(o, c, src).wait_send()

        @pl.when(root | (jnp.logical_not(near) & (lax.rem(c, 2) == core)))
        def _():
            sib_copy(o, c, src).wait_send()


def square_body(train_rows, train_labels, held_rows, held_labels, precision):
    rows, local = train_rows.shape
    nheld = held_rows.shape[0]
    n = lax.axis_size("dp")
    labels = train_labels.reshape(1, rows)
    hlabels = held_labels.reshape(1, nheld)
    vmem = pl.BlockSpec(memory_space=pltpu.VMEM)
    hbm = pl.BlockSpec(memory_space=pltpu.HBM)
    dma = pltpu.SemaphoreType.DMA
    cov, white, dist = pl.pallas_call(
        gather_kernel,
        out_shape=(
            jax.ShapeDtypeStruct((local, local), F32),
            jax.ShapeDtypeStruct((nheld, local), BF16),
            jax.ShapeDtypeStruct((1, nheld), F32),
        ),
        in_specs=[hbm, vmem, hbm, vmem, hbm],
        out_specs=(vmem, vmem, vmem),
        scratch_shapes=[
            pltpu.VMEM((rows, local), BF16),
            pltpu.VMEM(precision.shape, BF16),
            pltpu.VMEM((n, rows, local), BF16),
            pltpu.VMEM((n, rows, local), BF16),
            pltpu.VMEM((C, local), F32),
            pltpu.VMEM((C, local), F32),
            pltpu.VMEM((3 * C, local), BF16),
            pltpu.VMEM((3 * C, local), BF16),
            pltpu.VMEM((n, 8, rows), jnp.int32),
            pltpu.VMEM((nheld, local + 2 * BLK), BF16),
            pltpu.VMEM((C, local + 2 * BLK), BF16),
            pltpu.VMEM((C, local + 2 * BLK), BF16),
            pltpu.VMEM((nheld, local), F32),
            pltpu.VMEM((n, C, rows), BF16),
            pltpu.VMEM((nheld, C), BF16),
            pltpu.VMEM((nheld, 128), F32),
            pltpu.VMEM((8, nheld), F32),
            pltpu.VMEM((n, 8, nheld), F32),
            dma((n, CHUNKS)),
            dma((n, CHUNKS)),
            dma((n, CHUNKS)),
            dma((n, CHUNKS)),
            dma((n, CHUNKS)),
            dma((n, CHUNKS)),
            dma((n - 1,)),
            dma((n,)),
            dma((2,)),
            dma((2,)),
            dma((2, 2)),
            dma((2, 2)),
            dma((n - 1,)),
            dma((n,)),
            dma((n, CHUNKS)),
            dma((3,)),
        ],
        compiler_params=pltpu.CompilerParams(
            collective_id=0, has_side_effects=True, vmem_limit_bytes=40 * 1024 * 1024
        ),
    )(train_rows, labels, held_rows, hlabels, precision)
    return cov, white, dist.reshape(nheld)


def solution(mesh):
    square = mesh.shape["dp"] == 4 and mesh.shape["feat"] == 4
    return jax.shard_map(
        square_body if square else general_body,
        mesh=mesh,
        in_specs=(
            P(("layer", "dp"), "feat"),
            P(("layer", "dp"), None),
            P(("layer", "dp"), "feat"),
            P(("layer", "dp")),
            P("layer", "feat", None),
        ),
        out_specs=(P(("layer", "feat"), "dp"), P(("layer", "dp"), "feat"), P(("layer", "dp"))),
        check_vma=False,
    )
```
